32 devices in a mesh: blk: 32 (over z, y, x, core).
Axes of the slice: x: 2, y: 2, z: 4, core: 2. Of those that a mesh axis runs over, the one named last changes fastest.
Arguments:
- points: float32 [49152, 128], P('blk'), may hold values from -6 to 6
- inv_scale: float32 [128], replicated, may hold values from 0.03 to 0.3
- vectors: float32 [49152, 64], P('blk'), may hold values from -6 to 6
Outputs:
- product: float32 [49152, 64], P('blk')
The draws below stay inside these ranges and needn't reach their ends.
All inputs are finite; a program needn't handle non-finite values.
Results may differ from the reference program's by a relative error of at most 0.0003.
Values sent between devices are 32-bit elements; how exact they have to be, the bound alone decides.
A program may use at most 64 MiB of HBM per device.

```python
import math
import jax
import jax.numpy as jnp
from jax import lax

F = 128
R = 64
P_SIZE = 1536
STEPS = 2
NPTS = 49152
N_BLK = 32


def level_of(stream_key, shape, cuts, low, high):
    level, own = 1.0, jax.random.fold_in(stream_key, 6)
    for axis_at, blocks in cuts:
        steps = jnp.exp(jax.random.uniform(jax.random.fold_in(own, axis_at), (blocks,), jnp.float32, low / len(cuts), high / len(cuts)))
        level = level * jnp.repeat(steps, shape[axis_at] // blocks).reshape([-1 if axis == axis_at else 1 for axis in range(len(shape))])
    return level


def normal_values(rng, dims, deviation, most, shards=(), kind=jnp.bfloat16):
    gain = level_of(rng, dims, shards, -0.22, 0.18) if shards else 1.0
    array = jax.random.normal(rng, dims, jnp.float32) * deviation * gain
    return jnp.minimum(jnp.maximum(array, -most), most).astype(kind)


def setup_inputs(seed: int = 0) -> dict:
    key_of = jax.random.split(jax.random.key(seed), 4)
    return {
        "points": normal_values(key_of[0], (NPTS, F), 1.0, 6.0, ((0, 32),), jnp.float32),
        "inv_scale": jnp.clip(jnp.exp(jax.random.uniform(key_of[1], (F,), jnp.float32, math.log(0.03), math.log(0.3))), 0.03, 0.3),
        "vectors": normal_values(key_of[2], (NPTS, R), 1.0, 6.0, ((0, 32),), jnp.float32),
    }


def kernel_apply(left, left_sq, right, right_sq, vec):
    cross = jnp.dot(left, right.T, precision=lax.Precision.HIGHEST, preferred_element_type=jnp.float32)
    tile = jnp.exp(-0.5 * (left_sq[:, None] + right_sq[None, :] - 2.0 * cross))
    return jnp.dot(tile, vec, precision=lax.Precision.HIGHEST, preferred_element_type=jnp.float32)


def reference(points, inv_scale, vectors):
    scaled = (points * inv_scale[None, :]).reshape(N_BLK, P_SIZE, F)
    sq = jnp.sum(scaled * scaled, axis=2)
    blocks = vectors.reshape(N_BLK, P_SIZE, R)

    def one_block(index):
        total = jnp.zeros((P_SIZE, R), jnp.float32)
        for dist in range(-STEPS, STEPS + 1):
            other = ((index + dist) % N_BLK).astype(jnp.int32)
            total = total + kernel_apply(scaled[index], sq[index], scaled[other], sq[other], blocks[other])
        return total

    result = lax.map(one_block, jnp.arange(N_BLK, dtype=jnp.int32))
    return result.reshape(NPTS, R)
```

```python
import functools

import jax
import jax.numpy as jnp
from jax import lax
from jax.experimental import pallas as pl
from jax.experimental.pallas import tpu as pltpu
from jax.sharding import PartitionSpec as P

AXIS = "blk"
CHUNK = 256
OWN, MATE, FAR = 0, 1, 2
MESH = pl.DeviceIdType.MESH
F32, BF16 = jnp.float32, jnp.bfloat16


def split(x):
    high = x.astype(BF16)
    return high, (x - high.astype(F32)).astype(BF16)


def dot(a, b):
    return lax.dot_general(a, b, (((1,), (0,)), ((), ())), preferred_element_type=F32)


def dot_nt(a, b):
    return lax.dot_general(a, b, (((1,), (1,)), ((), ())), preferred_element_type=F32)


def fold(wide):
    half = wide.shape[0] // 2
    return wide[:half] + wide[half:]


def kernel(
    n, p_ref, s_ref, v_ref, o_ref,
    send, far_in, mate_in, left, right, vec, vec_t, sq_col, sq_row, acc_t, out_t,
    far_part, mate_part, far_back, mate_back,
    far_send_sem, far_recv_sem, mate_send_sem, mate_recv_sem,
    part_send_sem, part_recv_sem, mpart_send_sem, mpart_recv_sem,
):
    chunks = p_ref.shape[0] // CHUNK
    feat = p_ref.shape[1]
    cols = v_ref.shape[1]
    me = lax.axis_index(AXIS)
    odd = lax.rem(me, 2)
    even = odd == 0
    up, down = lax.rem(me + 2, n), lax.rem(me + n - 2, n)
    mate = me + 1 - 2 * odd
    host = jnp.where(even, down, up)
    guest = jnp.where(even, up, down)

    barrier = pltpu.get_barrier_semaphore()
    for other in (mate, up, down):
        pl.semaphore_signal(barrier, inc=1, device_id=(other,), device_id_type=MESH)

    def place(slot, c, scaled, vt):
        high, low = split(scaled)
        left[slot, c] = jnp.concatenate([high, low, high, low], axis=1)
        right[slot, c] = jnp.concatenate([high, low, low, high], axis=1)
        held = high.astype(F32) + low.astype(F32)
        squares = held * held
        sq_col[slot, c] = jnp.broadcast_to(
            -0.5 * jnp.sum(squares, axis=1, keepdims=True), (CHUNK, 128)
        )
        sq_row[slot, c] = jnp.broadcast_to(
            -0.5 * jnp.sum(squares.T, axis=0, keepdims=True), (8, CHUNK)
        )
        vt_high, vt_low = split(vt)
        vec_t[slot, c] = jnp.concatenate([vt_high, vt_low], axis=0)
        v_high, v_low = split(vt.T)
        vec[slot, c] = jnp.concatenate([v_high, v_low], axis=1)

    def place_packed(slot, c, source):
        scaled = source[c, :CHUNK]
        vt = jnp.concatenate(
            [source[c, CHUNK : CHUNK + cols], source[c, CHUNK + cols :]], axis=1
        )
        place(slot, c, scaled, vt)

    scale = s_ref[...]

    def prepare(c, carry):
        rows = pl.ds(pl.multiple_of(c * CHUNK, CHUNK), CHUNK)
        scaled = p_ref[rows, :] * scale
        vt = v_ref[rows, :].T
        send[c, :CHUNK] = scaled
        send[c, CHUNK : CHUNK + cols] = vt[:, :128]
        send[c, CHUNK + cols :] = vt[:, 128:]
        place(OWN, c, scaled, vt)
        return carry

    lax.fori_loop(0, chunks, prepare, 0)
    acc_t[...] = jnp.zeros_like(acc_t)

    pl.semaphore_wait(barrier, 3)

    def far_copy(c):
        return pltpu.make_async_remote_copy(
            src_ref=send.at[c], dst_ref=far_in.at[c],
            send_sem=far_send_sem.at[c], recv_sem=far_recv_sem.at[c],
            device_id=(host,), device_id_type=MESH,
        )

    def part_copy(c):
        return pltpu.make_async_remote_copy(
            src_ref=far_part.at[c], dst_ref=far_back.at[c],
            send_sem=part_send_sem.at[c], recv_sem=part_recv_sem.at[c],
            device_id=(guest,), device_id_type=MESH,
        )

    mate_copy = pltpu.make_async_remote_copy(
        src_ref=send, dst_ref=mate_in, send_sem=mate_send_sem, recv_sem=mate_recv_sem,
        device_id=(mate,), device_id_type=MESH,
    )
    mpart_copy = pltpu.make_async_remote_copy(
        src_ref=mate_part, dst_ref=mate_back, send_sem=mpart_send_sem,
        recv_sem=mpart_recv_sem, device_id=(mate,), device_id_type=MESH,
    )
    for c in range(chunks):
        far_copy(c).start()
    mate_copy.start()

    def tile(a, c, b, mirrored):
        rows = left[a, c]
        col = jnp.concatenate([sq_col[a, c]] * (CHUNK // 128), axis=1)
        rows_vec = vec_t[a, c]
        total = jnp.zeros((CHUNK, 2 * cols), F32)
        ahead = dot_nt(rows, right[b, 0])
        for j in range(chunks):
            cross = ahead
            if j + 1 < chunks:
                ahead = dot_nt(rows, right[b, j + 1])
            values = jnp.exp(cross + col + sq_row[b, j, 0:1])
            high, low = split(values)
            total = total + (dot(high, vec[b, j]) + dot(low, vec[b, j]))
            if mirrored:
                acc_t[b, j] += dot(rows_vec, high) + dot(rows_vec, low)
        return fold(total.T)

    def self_step(c, carry):
        out_t[c] = tile(OWN, c, OWN, False)
        return carry

    lax.fori_loop(0, chunks, self_step, 0)

    mate_copy.wait_recv()

    def place_mate(c, carry):
        place_packed(MATE, c, mate_in)
        return carry

    lax.fori_loop(0, chunks, place_mate, 0)

    def step(k, carry):
        second = lax.rem(k, 2)
        c = jnp.where(even, lax.rem(k, chunks), lax.div(k, 2))
        uses_far = jnp.logical_or(odd == 1, k >= chunks)
        a = jnp.where(uses_far, FAR, MATE)
        b = jnp.where(even, OWN, jnp.where(second == 0, MATE, OWN))
        arrives = jnp.where(even, k >= chunks, second == 0)

        @pl.when(arrives)
        def _():
            far_copy(c).wait_recv()
            place_packed(FAR, c, far_in)

        part = tile(a, c, b, True)

        @pl.when(jnp.logical_not(uses_far))
        def _():
            mate_part[c] = part

        @pl.when(jnp.logical_and(uses_far, arrives))
        def _():
            far_part[c] = part

        @pl.when(jnp.logical_and(uses_far, jnp.logical_not(arrives)))
        def _():
            far_part[c] += part

        @pl.when(jnp.where(even, k >= chunks, second == 1))
        def _():
            part_copy(c).start()

        @pl.when(jnp.logical_and(even, k == chunks - 1))
        def _():
            mpart_copy.start()

        return carry

    lax.fori_loop(0, 2 * chunks, step, 0)

    @pl.when(odd == 1)
    def _():
        for c in range(chunks):
            mate_part[c] = fold(acc_t[MATE, c])
        mpart_copy.start()

    for c in range(chunks):
        out_t[c] += fold(acc_t[OWN, c])
    mpart_copy.wait_recv()
    for c in range(chunks):
        part_copy(c).wait_recv()
        o_ref[c * CHUNK : (c + 1) * CHUNK, :] = (out_t[c] + mate_back[c] + far_back[c]).T
    for c in range(chunks):
        far_copy(c).wait_send()
        part_copy(c).wait_send()
    mate_copy.wait_send()
    mpart_copy.wait_send()


def per_device(points, inv_scale, vectors):
    n = lax.axis_size(AXIS)
    rows, feat = points.shape
    cols = vectors.shape[1]
    chunks = rows // CHUNK
    packed = (chunks, CHUNK + 2 * cols, 128)
    turned = (chunks, cols, CHUNK)
    vmem = pl.BlockSpec(memory_space=pltpu.VMEM)
    sem = pltpu.SemaphoreType.DMA
    return pl.pallas_call(
        functools.partial(kernel, n),
        out_shape=jax.ShapeDtypeStruct((rows, cols), F32),
        in_specs=[vmem] * 3,
        out_specs=vmem,
        scratch_shapes=[
            pltpu.VMEM(packed, F32),
            pltpu.VMEM(packed, F32),
            pltpu.VMEM(packed, F32),
            pltpu.VMEM((3, chunks, CHUNK, 4 * feat), BF16),
            pltpu.VMEM((3, chunks, CHUNK, 4 * feat), BF16),
            pltpu.VMEM((3, chunks, CHUNK, 2 * cols), BF16),
            pltpu.VMEM((3, chunks, 2 * cols, CHUNK), BF16),
            pltpu.VMEM((3, chunks, CHUNK, 128), F32),
            pltpu.VMEM((3, chunks, 8, CHUNK), F32),
            pltpu.VMEM((2, chunks, 2 * cols, CHUNK), F32),
            pltpu.VMEM(turned, F32),
            pltpu.VMEM(turned, F32),
            pltpu.VMEM(turned, F32),
            pltpu.VMEM(turned, F32),
            pltpu.VMEM(turned, F32),
            sem((chunks,)), sem((chunks,)), sem, sem,
            sem((chunks,)), sem((chunks,)), sem, sem,
        ],
        compiler_params=pltpu.CompilerParams(
            collective_id=0, has_side_effects=True, vmem_limit_bytes=48 * 1024 * 1024
        ),
    )(points, inv_scale[None, :], vectors)


def solution(mesh):
    return jax.shard_map(
        per_device, mesh=mesh,
        in_specs=(P(AXIS, None), P(), P(AXIS, None)), out_specs=P(AXIS, None),
        check_vma=False,
    )
```

```python
import functools

import jax
import jax.numpy as jnp
from jax import lax
from jax.experimental import pallas as pl
from jax.experimental.pallas import tpu as pltpu
from jax.sharding import PartitionSpec as P

AXIS = "blk"
CHUNK = 512
STRIP = 256
LOG2E_ROOT = 1.2011224087864498
OWN, MATE, FAR = 0, 1, 2
MESH = pl.DeviceIdType.MESH
F32, BF16 = jnp.float32, jnp.bfloat16


def split(x):
    high = x.astype(BF16)
    return high, (x - high.astype(F32)).astype(BF16)


def dot(a, b):
    return lax.dot_general(a, b, (((1,), (0,)), ((), ())), preferred_element_type=F32)


def dot_nt(a, b):
    return lax.dot_general(a, b, (((1,), (1,)), ((), ())), preferred_element_type=F32)


def fold(wide):
    half = wide.shape[0] // 2
    return wide[:half] + wide[half:]


def kernel(
    n, p_ref, s_ref, v_ref, o_ref,
    send, far_in, mate_in, left, right, vec, vec_t, sq_col, sq_row, acc_t, out_t,
    far_part, mate_part, far_back, mate_back,
    far_send_sem, far_recv_sem, mate_send_sem, mate_recv_sem,
    part_send_sem, part_recv_sem, mpart_send_sem, mpart_recv_sem,
):
    chunks = p_ref.shape[0] // CHUNK
    cols = v_ref.shape[0]
    strips, lanes = CHUNK // STRIP, CHUNK // 128
    me = lax.axis_index(AXIS)
    odd = lax.rem(me, 2)
    even = odd == 0
    up, down = lax.rem(me + 2, n), lax.rem(me + n - 2, n)
    mate = me + 1 - 2 * odd
    host = jnp.where(even, down, up)
    guest = jnp.where(even, up, down)

    barrier = pltpu.get_barrier_semaphore()
    for other in (mate, up, down):
        pl.semaphore_signal(barrier, inc=1, device_id=(other,), device_id_type=MESH)

    def place(slot, c, scaled, vt):
        high, low = split(scaled)
        left[slot, c] = jnp.concatenate([high, low, high, low], axis=1)
        turned = jnp.concatenate([high, low, low, high], axis=1)
        held = high.astype(F32) + low.astype(F32)
        squares = held * held
        sq_col[slot, c] = jnp.broadcast_to(
            -0.5 * jnp.sum(squares, axis=1, keepdims=True), (CHUNK, 128)
        )
        row = -0.5 * jnp.sum(squares.T, axis=0, keepdims=True)
        vt_high, vt_low = split(vt)
        wide = jnp.concatenate([vt_high, vt_low], axis=0)
        vec_t[slot, c] = jnp.concatenate([wide, wide], axis=1)
        v_high, v_low = split(vt.T)
        tall = jnp.concatenate([v_high, v_low], axis=1)
        for h in range(strips):
            part = slice(h * STRIP, (h + 1) * STRIP)
            j = c * strips + h
            right[slot, j] = turned[part]
            sq_row[slot, j] = jnp.broadcast_to(row[:, part], (8, STRIP))
            vec[slot, j] = jnp.concatenate([tall[part], tall[part]], axis=0)

    def place_packed(slot, c, source):
        pieces = [source[c, CHUNK + q * cols : CHUNK + (q + 1) * cols] for q in range(lanes)]
        place(slot, c, source[c, :CHUNK], jnp.concatenate(pieces, axis=1))

    scale = s_ref[...] * LOG2E_ROOT

    def pack(c, carry):
        rows = pl.ds(pl.multiple_of(c * CHUNK, CHUNK), CHUNK)
        send[c, :CHUNK] = p_ref[rows, :] * scale
        vt = v_ref[:, rows]
        for q in range(lanes):
            send[c, CHUNK + q * cols : CHUNK + (q + 1) * cols] = vt[:, q * 128 : (q + 1) * 128]
        return carry

    lax.fori_loop(0, chunks, pack, 0)
    pl.semaphore_wait(barrier, 3)

    def far_copy(c):
        return pltpu.make_async_remote_copy(
            src_ref=send.at[c], dst_ref=far_in.at[c],
            send_sem=far_send_sem.at[c], recv_sem=far_recv_sem.at[c],
            device_id=(host,), device_id_type=MESH,
        )

    def part_copy(c):
        return pltpu.make_async_remote_copy(
            src_ref=far_part.at[c], dst_ref=far_back.at[c],
            send_sem=part_send_sem.at[c], recv_sem=part_recv_sem.at[c],
            device_id=(guest,), device_id_type=MESH,
        )

    mate_copy = pltpu.make_async_remote_copy(
        src_ref=send, dst_ref=mate_in, send_sem=mate_send_sem, recv_sem=mate_recv_sem,
        device_id=(mate,), device_id_type=MESH,
    )
    mpart_copy = pltpu.make_async_remote_copy(
        src_ref=mate_part, dst_ref=mate_back, send_sem=mpart_send_sem,
        recv_sem=mpart_recv_sem, device_id=(mate,), device_id_type=MESH,
    )
    for c in range(chunks):
        far_copy(c).start()
    mate_copy.start()

    def place_own(c, carry):
        place_packed(OWN, c, send)
        return carry

    lax.fori_loop(0, chunks, place_own, 0)
    acc_t[...] = jnp.zeros_like(acc_t)

    def tile(a, c, b, mirrored):
        rows = left[a, c]
        col = jnp.concatenate([sq_col[a, c]] * (STRIP // 128), axis=1)
        count = chunks * strips
        crosses, halves = {}, {}
        total = jnp.zeros((CHUNK, 2 * cols), F32)
        for j in range(count + 2):
            if j < count:
                crosses[j] = dot_nt(rows, right[b, j])
            if 2 <= j:
                high, low = halves.pop(j - 2)
                total = total + dot(jnp.concatenate([high, low], axis=1), vec[b, j - 2])
                if mirrored:
                    acc_t[b, j - 2] += dot(vec_t[a, c], jnp.concatenate([high, low], axis=0))
            if 1 <= j <= count:
                cross = crosses.pop(j - 1)
                halves[j - 1] = split(jnp.exp2(cross + col + sq_row[b, j - 1, 0:1]))
        return fold(total.T)

    def self_step(c, carry):
        out_t[c] = tile(OWN, c, OWN, False)
        return carry

    lax.fori_loop(0, chunks, self_step, 0)

    mate_copy.wait_recv()

    def place_mate(c, carry):
        place_packed(MATE, c, mate_in)
        return carry

    lax.fori_loop(0, chunks, place_mate, 0)

    def step(k, carry):
        second = lax.rem(k, 2)
        c = jnp.where(even, lax.rem(k, chunks), lax.div(k, 2))
        uses_far = jnp.logical_or(odd == 1, k >= chunks)
        a = jnp.where(uses_far, FAR, MATE)
        b = jnp.where(even, OWN, jnp.where(second == 0, MATE, OWN))
        arrives = jnp.where(even, k >= chunks, second == 0)

        @pl.when(arrives)
        def _():
            far_copy(c).wait_recv()
            place_packed(FAR, c, far_in)

        part = tile(a, c, b, True)

        @pl.when(jnp.logical_not(uses_far))
        def _():
            mate_part[c] = part

        @pl.when(jnp.logical_and(uses_far, arrives))
        def _():
            far_part[c] = part

        @pl.when(jnp.logical_and(uses_far, jnp.logical_not(arrives)))
        def _():
            far_part[c] += part

        @pl.when(jnp.where(even, k >= chunks, second == 1))
        def _():
            part_copy(c).start()

        @pl.when(jnp.logical_and(even, k == chunks - 1))
        def _():
            mpart_copy.start()

        return carry

    lax.fori_loop(0, 2 * chunks, step, 0)

    def mirror_of(b, c):
        pieces = [fold(acc_t[b, c * strips + h]) for h in range(strips)]
        return jnp.concatenate(pieces, axis=1)

    @pl.when(odd == 1)
    def _():
        for c in range(chunks):
            mate_part[c] = mirror_of(MATE, c)
        mpart_copy.start()

    for c in range(chunks):
        out_t[c] += mirror_of(OWN, c)
    mpart_copy.wait_recv()
    for c in range(chunks):
        part_copy(c).wait_recv()
        o_ref[:, c * CHUNK : (c + 1) * CHUNK] = out_t[c] + mate_back[c] + far_back[c]
    for c in range(chunks):
        far_copy(c).wait_send()
        part_copy(c).wait_send()
    mate_copy.wait_send()
    mpart_copy.wait_send()


def per_device(points, inv_scale, vectors):
    n = lax.axis_size(AXIS)
    rows, feat = points.shape
    cols = vectors.shape[1]
    chunks = rows // CHUNK
    strips = rows // STRIP
    packed = (chunks, CHUNK + CHUNK // 128 * cols, 128)
    turned = (chunks, cols, CHUNK)
    vmem = pl.BlockSpec(memory_space=pltpu.VMEM)
    sem = pltpu.SemaphoreType.DMA
    return pl.pallas_call(
        functools.partial(kernel, n),
        out_shape=jax.ShapeDtypeStruct((cols, rows), F32),
        in_specs=[vmem] * 3,
        out_specs=vmem,
        scratch_shapes=[
            pltpu.VMEM(packed, F32),
            pltpu.VMEM(packed, F32),
            pltpu.VMEM(packed, F32),
            pltpu.VMEM((3, chunks, CHUNK, 4 * feat), BF16),
            pltpu.VMEM((3, strips, STRIP, 4 * feat), BF16),
            pltpu.VMEM((3, strips, 2 * STRIP, 2 * cols), BF16),
            pltpu.VMEM((3, chunks, 2 * cols, 2 * CHUNK), BF16),
            pltpu.VMEM((3, chunks, CHUNK, 128), F32),
            pltpu.VMEM((3, strips, 8, STRIP), F32),
            pltpu.VMEM((2, strips, 2 * cols, STRIP), F32),
            pltpu.VMEM(turned, F32),
            pltpu.VMEM(turned, F32),
            pltpu.VMEM(turned, F32),
            pltpu.VMEM(turned, F32),
            pltpu.VMEM(turned, F32),
            sem((chunks,)), sem((chunks,)), sem, sem,
            sem((chunks,)), sem((chunks,)), sem, sem,
        ],
        compiler_params=pltpu.CompilerParams(
            collective_id=0, has_side_effects=True, vmem_limit_bytes=48 * 1024 * 1024
        ),
    )(points, inv_scale[None, :], vectors.T).T


def solution(mesh):
    return jax.shard_map(
        per_device, mesh=mesh,
        in_specs=(P(AXIS, None), P(), P(AXIS, None)), out_specs=P(AXIS, None),
        check_vma=False,
    )
```

```python
import functools

import jax
import jax.numpy as jnp
from jax import lax
from jax.experimental import pallas as pl
from jax.experimental.pallas import tpu as pltpu
from jax.sharding import PartitionSpec as P

AXIS = "blk"
CHUNK = 512
STRIP = 256
LOG2E_ROOT = 1.2011224087864498
OWN, MATE, FAR = 0, 1, 2
MESH = pl.DeviceIdType.MESH
F32, BF16 = jnp.float32, jnp.bfloat16


def split(x):
    high = x.astype(BF16)
    return high, (x - high.astype(F32)).astype(BF16)


def dot(a, b):
    return lax.dot_general(a, b, (((1,), (0,)), ((), ())), preferred_element_type=F32)


def dot_nt(a, b):
    return lax.dot_general(a, b, (((1,), (1,)), ((), ())), preferred_element_type=F32)


def fold(wide):
    half = wide.shape[0] // 2
    return wide[:half] + wide[half:]


def kernel(
    n, p_ref, s_ref, v_ref, o_ref,
    send, far_in, mate_in, left, right, vec, sq_col, sq_row, acc_t, out_t,
    far_part, mate_part, far_back, mate_back,
    far_send_sem, far_recv_sem, mate_send_sem, mate_recv_sem,
    part_send_sem, part_recv_sem, mpart_send_sem, mpart_recv_sem,
):
    chunks = p_ref.shape[0] // CHUNK
    cols = v_ref.shape[0]
    strips, lanes = CHUNK // STRIP, CHUNK // 128
    me = lax.axis_index(AXIS)
    odd = lax.rem(me, 2)
    even = odd == 0
    up, down = lax.rem(me + 2, n), lax.rem(me + n - 2, n)
    mate = me + 1 - 2 * odd
    host = jnp.where(even, down, up)
    guest = jnp.where(even, up, down)

    barrier = pltpu.get_barrier_semaphore()
    for other in (mate, guest):
        pl.semaphore_signal(barrier, inc=1, device_id=(other,), device_id_type=MESH)

    def place(slot, c, scaled, vt):
        high, low = split(scaled)
        left[slot, c] = jnp.concatenate([high, low, high, low], axis=1)
        turned = jnp.concatenate([high, low, low, high], axis=1)
        held = high.astype(F32) + low.astype(F32)
        squares = held * held
        sq_col[slot, c] = jnp.broadcast_to(
            -0.5 * jnp.sum(squares, axis=1, keepdims=True), (CHUNK, 128)
        )
        row = -0.5 * jnp.sum(squares.T, axis=0, keepdims=True)
        v_high, v_low = split(vt.T)
        tall = jnp.concatenate([v_high, v_low], axis=1)
        for h in range(strips):
            part = slice(h * STRIP, (h + 1) * STRIP)
            j = c * strips + h
            right[slot, j] = turned[part]
            sq_row[slot, j] = jnp.broadcast_to(row[:, part], (8, STRIP))
            vec[slot, j] = jnp.concatenate([tall[part], tall[part]], axis=0)

    def place_packed(slot, c, source):
        pieces = [source[c, CHUNK + q * cols : CHUNK + (q + 1) * cols] for q in range(lanes)]
        place(slot, c, source[c, :CHUNK], jnp.concatenate(pieces, axis=1))

    scale = s_ref[...] * LOG2E_ROOT

    def pack(c, carry):
        rows = pl.ds(pl.multiple_of(c * CHUNK, CHUNK), CHUNK)
        send[c, :CHUNK] = p_ref[rows, :] * scale
        vt = v_ref[:, rows]
        for q in range(lanes):
            send[c, CHUNK + q * cols : CHUNK + (q + 1) * cols] = vt[:, q * 128 : (q + 1) * 128]
        return carry

    lax.fori_loop(0, chunks, pack, 0)
    pl.semaphore_wait(barrier, 2)

    def far_copy(c):
        return pltpu.make_async_remote_copy(
            src_ref=send.at[c], dst_ref=far_in.at[c],
            send_sem=far_send_sem.at[c], recv_sem=far_recv_sem.at[c],
            device_id=(host,), device_id_type=MESH,
        )

    def part_copy(c):
        return pltpu.make_async_remote_copy(
            src_ref=far_part.at[c], dst_ref=far_back.at[c],
            send_sem=part_send_sem.at[c], recv_sem=part_recv_sem.at[c],
            device_id=(guest,), device_id_type=MESH,
        )

    mate_copy = pltpu.make_async_remote_copy(
        src_ref=send, dst_ref=mate_in, send_sem=mate_send_sem, recv_sem=mate_recv_sem,
        device_id=(mate,), device_id_type=MESH,
    )
    mpart_copy = pltpu.make_async_remote_copy(
        src_ref=mate_part, dst_ref=mate_back, send_sem=mpart_send_sem,
        recv_sem=mpart_recv_sem, device_id=(mate,), device_id_type=MESH,
    )
    @pl.when(odd == 1)
    def _():
        for c in range(chunks):
            far_copy(c).start()

    mate_copy.start()

    def place_own(c, carry):
        place_packed(OWN, c, send)
        return carry

    lax.fori_loop(0, chunks, place_own, 0)
    acc_t[...] = jnp.zeros_like(acc_t)

    def tile(a, c, b, mirrored):
        rows = left[a, c]
        col = jnp.concatenate([sq_col[a, c]] * (STRIP // 128), axis=1)
        count = chunks * strips
        crosses, halves = {}, {}
        total = jnp.zeros((CHUNK, 2 * cols), F32)
        for j in range(count + 2):
            if j < count:
                crosses[j] = dot_nt(rows, right[b, j])
            if 2 <= j:
                high, low = halves.pop(j - 2)
                total = total + dot(jnp.concatenate([high, low], axis=1), vec[b, j - 2])
                if mirrored:
                    turned = []
                    for h in range(strips):
                        part = slice(h * STRIP, (h + 1) * STRIP)
                        turned += [high[part].T, low[part].T]
                    weights = jnp.concatenate([vec[a, c * strips + h] for h in range(strips)], axis=0)
                    acc_t[b, j - 2] += dot(jnp.concatenate(turned, axis=1), weights)
            if 1 <= j <= count:
                cross = crosses.pop(j - 1)
                halves[j - 1] = split(jnp.exp2(cross + col + sq_row[b, j - 1, 0:1]))
        return fold(total.T)

    def self_step(c, carry):
        out_t[c] = tile(OWN, c, OWN, False)

        @pl.when(even)
        def _():
            far_copy(c).start()

        return carry

    lax.fori_loop(0, chunks, self_step, 0)

    mate_copy.wait_recv()

    def place_mate(c, carry):
        place_packed(MATE, c, mate_in)
        return carry

    lax.fori_loop(0, chunks, place_mate, 0)

    def step(k, carry):
        second = lax.rem(k, 2)
        c = jnp.where(even, lax.rem(k, chunks), lax.div(k, 2))
        uses_far = jnp.logical_or(odd == 1, k >= chunks)
        a = jnp.where(uses_far, FAR, MATE)
        b = jnp.where(even, OWN, jnp.where(second == 0, MATE, OWN))
        arrives = jnp.where(even, k >= chunks, second == 0)

        @pl.when(arrives)
        def _():
            far_copy(c).wait_recv()
            place_packed(FAR, c, far_in)

        part = tile(a, c, b, True)

        @pl.when(jnp.logical_not(uses_far))
        def _():
            mate_part[c] = part

        @pl.when(jnp.logical_and(uses_far, arrives))
        def _():
            far_part[c] = part

        @pl.when(jnp.logical_and(uses_far, jnp.logical_not(arrives)))
        def _():
            far_part[c] += part

        @pl.when(jnp.where(even, k >= chunks, second == 1))
        def _():
            part_copy(c).start()

        @pl.when(jnp.logical_and(even, k == chunks - 1))
        def _():
            mpart_copy.start()

        return carry

    lax.fori_loop(0, 2 * chunks, step, 0)

    def mirror_of(b, c):
        pieces = [fold(acc_t[b, c * strips + h].T) for h in range(strips)]
        return jnp.concatenate(pieces, axis=1)

    @pl.when(odd == 1)
    def _():
        for c in range(chunks):
            mate_part[c] = mirror_of(MATE, c)
        mpart_copy.start()

    for c in range(chunks):
        out_t[c] += mirror_of(OWN, c)
    mpart_copy.wait_recv()
    for c in range(chunks):
        part_copy(c).wait_recv()
        o_ref[:, c * CHUNK : (c + 1) * CHUNK] = out_t[c] + mate_back[c] + far_back[c]
    for c in range(chunks):
        far_copy(c).wait_send()
        part_copy(c).wait_send()
    mate_copy.wait_send()
    mpart_copy.wait_send()


def per_device(points, inv_scale, vectors):
    n = lax.axis_size(AXIS)
    rows, feat = points.shape
    cols = vectors.shape[1]
    chunks = rows // CHUNK
    strips = rows // STRIP
    packed = (chunks, CHUNK + CHUNK // 128 * cols, 128)
    turned = (chunks, cols, CHUNK)
    vmem = pl.BlockSpec(memory_space=pltpu.VMEM)
    sem = pltpu.SemaphoreType.DMA
    return pl.pallas_call(
        functools.partial(kernel, n),
        out_shape=jax.ShapeDtypeStruct((cols, rows), F32),
        in_specs=[vmem] * 3,
        out_specs=vmem,
        scratch_shapes=[
            pltpu.VMEM(packed, F32),
            pltpu.VMEM(packed, F32),
            pltpu.VMEM(packed, F32),
            pltpu.VMEM((3, chunks, CHUNK, 4 * feat), BF16),
            pltpu.VMEM((3, strips, STRIP, 4 * feat), BF16),
            pltpu.VMEM((3, strips, 2 * STRIP, 2 * cols), BF16),
            pltpu.VMEM((3, chunks, CHUNK, 128), F32),
            pltpu.VMEM((3, strips, 8, STRIP), F32),
            pltpu.VMEM((2, strips, STRIP, 2 * cols), F32),
            pltpu.VMEM(turned, F32),
            pltpu.VMEM(turned, F32),
            pltpu.VMEM(turned, F32),
            pltpu.VMEM(turned, F32),
            pltpu.VMEM(turned, F32),
            sem((chunks,)), sem((chunks,)), sem, sem,
            sem((chunks,)), sem((chunks,)), sem, sem,
        ],
        compiler_params=pltpu.CompilerParams(
            collective_id=0, has_side_effects=True, vmem_limit_bytes=48 * 1024 * 1024
        ),
    )(points, inv_scale[None, :], vectors.T).T


def solution(mesh):
    return jax.shard_map(
        per_device, mesh=mesh,
        in_specs=(P(AXIS, None), P(), P(AXIS, None)), out_specs=P(AXIS, None),
        check_vma=False,
    )
```

```python
import functools

import jax
import jax.numpy as jnp
from jax import lax
from jax.experimental import pallas as pl
from jax.experimental.pallas import tpu as pltpu
from jax.sharding import PartitionSpec as P

AXIS = "blk"
CHUNK = 512
STRIP = 256
LOG2E_ROOT = 1.2011224087864498
OWN, MATE, FAR = 0, 1, 2
MESH = pl.DeviceIdType.MESH
F32, BF16 = jnp.float32, jnp.bfloat16


def split(x):
    high = x.astype(BF16)
    return high, (x - high.astype(F32)).astype(BF16)


def dot(a, b):
    return lax.dot_general(a, b, (((1,), (0,)), ((), ())), preferred_element_type=F32)


def dot_nt(a, b):
    return lax.dot_general(a, b, (((1,), (1,)), ((), ())), preferred_element_type=F32)


def fold(wide):
    half = wide.shape[0] // 2
    return wide[:half] + wide[half:]


def kernel(
    n, p_ref, s_ref, v_ref, o_ref,
    send, far_in, mate_in, left, right, vec, vec_t, sq_col, sq_row, acc_t, out_t,
    cross, tile_high, tile_low, scale_in,
    far_part, mate_part, far_back, mate_back,
    load_sem, scale_sem, far_send_sem, far_recv_sem, mate_send_sem, mate_recv_sem,
    part_send_sem, part_recv_sem, mpart_send_sem, mpart_recv_sem,
):
    chunks = p_ref.shape[0] // CHUNK
    cols = v_ref.shape[0]
    strips, lanes = CHUNK // STRIP, CHUNK // 128
    me = lax.axis_index(AXIS)
    odd = lax.rem(me, 2)
    even = odd == 0
    up, down = lax.rem(me + 2, n), lax.rem(me + n - 2, n)
    mate = me + 1 - 2 * odd
    host = jnp.where(even, down, up)
    guest = jnp.where(even, up, down)

    barrier = pltpu.get_barrier_semaphore()

    def load_parts(c):
        pairs = [(p_ref.at[c * CHUNK : (c + 1) * CHUNK], send.at[c, 0:CHUNK])]
        for q in range(lanes):
            first = c * CHUNK + q * 128
            at = CHUNK + q * cols
            pairs.append((v_ref.at[:, first : first + 128], send.at[c, at : at + cols]))
        return [
            pltpu.make_async_copy(src, dst, load_sem.at[c, i])
            for i, (src, dst) in enumerate(pairs)
        ]

    loads = [load_parts(c) for c in range(chunks)]
    scale_load = pltpu.make_async_copy(s_ref, scale_in, scale_sem)
    scale_load.start()
    for group in loads:
        for copy in group:
            copy.start()
    for other in (mate, guest):
        pl.semaphore_signal(barrier, inc=1, device_id=(other,), device_id_type=MESH)

    def place(slot, c, source):
        rows = pl.ds(pl.multiple_of(c * CHUNK, CHUNK), CHUNK)
        pieces = [source[c, CHUNK + q * cols : CHUNK + (q + 1) * cols] for q in range(lanes)]
        high, low = split(source[c, :CHUNK])
        left[slot, c] = jnp.concatenate([high, low, high, low], axis=1)
        right[slot, rows] = jnp.concatenate([high, low, low, high], axis=1)
        held = high.astype(F32) + low.astype(F32)
        squares = held * held
        sq_col[slot, c] = jnp.broadcast_to(
            -0.5 * jnp.sum(squares, axis=1, keepdims=True), (CHUNK, 128)
        )
        row = -0.5 * jnp.sum(squares.T, axis=0, keepdims=True)
        sq_row[slot, :, rows] = jnp.broadcast_to(row, (8, CHUNK))
        vt = jnp.concatenate(pieces, axis=1)
        vec_t[slot, c] = jnp.concatenate(split(vt), axis=0)
        vec[slot, rows] = jnp.concatenate(split(vt.T), axis=1)

    scale_load.wait()
    scale = scale_in[...] * LOG2E_ROOT
    for c in range(chunks):
        for copy in loads[c]:
            copy.wait()
        send[c, :CHUNK] = send[c, :CHUNK] * scale
    pl.semaphore_wait(barrier, 2)

    def far_copy(c):
        return pltpu.make_async_remote_copy(
            src_ref=send.at[c], dst_ref=far_in.at[c],
            send_sem=far_send_sem.at[c], recv_sem=far_recv_sem.at[c],
            device_id=(host,), device_id_type=MESH,
        )

    def part_copy(c):
        return pltpu.make_async_remote_copy(
            src_ref=far_part.at[c], dst_ref=far_back.at[c],
            send_sem=part_send_sem.at[c], recv_sem=part_recv_sem.at[c],
            device_id=(guest,), device_id_type=MESH,
        )

    mate_copy = pltpu.make_async_remote_copy(
        src_ref=send, dst_ref=mate_in, send_sem=mate_send_sem, recv_sem=mate_recv_sem,
        device_id=(mate,), device_id_type=MESH,
    )
    mpart_copy = pltpu.make_async_remote_copy(
        src_ref=mate_part, dst_ref=mate_back, send_sem=mpart_send_sem,
        recv_sem=mpart_recv_sem, device_id=(mate,), device_id_type=MESH,
    )
    @pl.when(odd == 1)
    def _():
        for c in range(chunks):
            far_copy(c).start()

    mate_copy.start()

    def place_own(c, carry):
        place(OWN, c, send)
        return carry

    lax.fori_loop(0, chunks, place_own, 0)
    acc_t[...] = jnp.zeros_like(acc_t)

    def tile(a, c, b, mirrored):
        col = jnp.concatenate([sq_col[a, c]] * (STRIP // 128), axis=1)
        cross[...] = dot_nt(left[a, c], right[b])
        for j in range(chunks * strips):
            at = slice(j * STRIP, (j + 1) * STRIP)
            values = jnp.exp2(cross[:, at] + col + sq_row[b, 0:1, at])
            tile_high[:, at], tile_low[:, at] = split(values)
        total = dot(tile_high[...], vec[b]) + dot(tile_low[...], vec[b])
        if mirrored:
            acc_t[b] += dot(vec_t[a, c], tile_high[...]) + dot(vec_t[a, c], tile_low[...])
        return fold(total.T)

    def self_step(c, carry):
        out_t[c] = tile(OWN, c, OWN, False)

        @pl.when(even)
        def _():
            far_copy(c).start()

        return carry

    lax.fori_loop(0, chunks, self_step, 0)

    mate_copy.wait_recv()

    def place_mate(c, carry):
        place(MATE, c, mate_in)
        return carry

    lax.fori_loop(0, chunks, place_mate, 0)

    def step(k, carry):
        second = lax.rem(k, 2)
        c = jnp.where(even, lax.rem(k, chunks), lax.div(k, 2))
        uses_far = jnp.logical_or(odd == 1, k >= chunks)
        a = jnp.where(uses_far, FAR, MATE)
        b = jnp.where(even, OWN, jnp.where(second == 0, MATE, OWN))
        arrives = jnp.where(even, k >= chunks, second == 0)

        @pl.when(arrives)
        def _():
            far_copy(c).wait_recv()
            place(FAR, c, far_in)

        part = tile(a, c, b, True)

        @pl.when(jnp.logical_not(uses_far))
        def _():
            mate_part[c] = part

        @pl.when(jnp.logical_and(uses_far, arrives))
        def _():
            far_part[c] = part

        @pl.when(jnp.logical_and(uses_far, jnp.logical_not(arrives)))
        def _():
            far_part[c] += part

        @pl.when(jnp.where(even, k >= chunks, second == 1))
        def _():
            part_copy(c).start()

        @pl.when(jnp.logical_and(even, k == chunks - 1))
        def _():
            mpart_copy.start()

        return carry

    lax.fori_loop(0, 2 * chunks, step, 0)

    def mirror_of(b, c):
        return fold(acc_t[b, :, c * CHUNK : (c + 1) * CHUNK])

    @pl.when(odd == 1)
    def _():
        for c in range(chunks):
            mate_part[c] = mirror_of(MATE, c)
        mpart_copy.start()

    for c in range(chunks):
        out_t[c] += mirror_of(OWN, c)
    mpart_copy.wait_recv()
    for c in range(chunks):
        part_copy(c).wait_recv()
        o_ref[:, c * CHUNK : (c + 1) * CHUNK] = out_t[c] + mate_back[c] + far_back[c]
    for c in range(chunks):
        far_copy(c).wait_send()
        part_copy(c).wait_send()
    mate_copy.wait_send()
    mpart_copy.wait_send()


def per_device(points, inv_scale, vectors):
    n = lax.axis_size(AXIS)
    rows, feat = points.shape
    cols = vectors.shape[1]
    chunks = rows // CHUNK
    packed = (chunks, CHUNK + CHUNK // 128 * cols, 128)
    turned = (chunks, cols, CHUNK)
    vmem = pl.BlockSpec(memory_space=pltpu.VMEM)
    sem = pltpu.SemaphoreType.DMA
    return pl.pallas_call(
        functools.partial(kernel, n),
        out_shape=jax.ShapeDtypeStruct((cols, rows), F32),
        in_specs=[pl.BlockSpec(memory_space=pl.ANY)] * 3,
        out_specs=vmem,
        scratch_shapes=[
            pltpu.VMEM(packed, F32),
            pltpu.VMEM(packed, F32),
            pltpu.VMEM(packed, F32),
            pltpu.VMEM((3, chunks, CHUNK, 4 * feat), BF16),
            pltpu.VMEM((3, rows, 4 * feat), BF16),
            pltpu.VMEM((3, rows, 2 * cols), BF16),
            pltpu.VMEM((3, chunks, 2 * cols, CHUNK), BF16),
            pltpu.VMEM((3, chunks, CHUNK, 128), F32),
            pltpu.VMEM((3, 8, rows), F32),
            pltpu.VMEM((2, 2 * cols, rows), F32),
            pltpu.VMEM(turned, F32),
            pltpu.VMEM((CHUNK, rows), F32),
            pltpu.VMEM((CHUNK, rows), BF16),
            pltpu.VMEM((CHUNK, rows), BF16),
            pltpu.VMEM((1, feat), F32),
            pltpu.VMEM(turned, F32),
            pltpu.VMEM(turned, F32),
            pltpu.VMEM(turned, F32),
            pltpu.VMEM(turned, F32),
            sem((chunks, 1 + CHUNK // 128)), sem,
            sem((chunks,)), sem((chunks,)), sem, sem,
            sem((chunks,)), sem((chunks,)), sem, sem,
        ],
        compiler_params=pltpu.CompilerParams(
            collective_id=0, has_side_effects=True, vmem_limit_bytes=48 * 1024 * 1024
        ),
    )(points, inv_scale[None, :], vectors.T).T


def solution(mesh):
    return jax.shard_map(
        per_device, mesh=mesh,
        in_specs=(P(AXIS, None), P(), P(AXIS, None)), out_specs=P(AXIS, None),
        check_vma=False,
    )
```

```python
import functools

import jax
import jax.numpy as jnp
from jax import lax
from jax.experimental import pallas as pl
from jax.experimental.pallas import tpu as pltpu
from jax.sharding import PartitionSpec as P

AXIS = "blk"
CHUNK = 512
STRIP = 256
LOG2E_ROOT = 1.2011224087864498
OWN, MATE, FAR = 0, 1, 2
MESH = pl.DeviceIdType.MESH
F32, BF16 = jnp.float32, jnp.bfloat16


def split(x):
    high = x.astype(BF16)
    return high, (x - high.astype(F32)).astype(BF16)


def dot(a, b):
    return lax.dot_general(a, b, (((1,), (0,)), ((), ())), preferred_element_type=F32)


def dot_nt(a, b):
    return lax.dot_general(a, b, (((1,), (1,)), ((), ())), preferred_element_type=F32)


def fold(wide):
    half = wide.shape[0] // 2
    return wide[:half] + wide[half:]


def kernel(
    n, p_ref, s_ref, v_ref, o_ref,
    send, far_in, mate_in, relay_in, left, right, vec, vec_t, sq_col, sq_row, acc_t, out_t,
    cross, tile_high, tile_low, scale_in,
    far_part, mate_part, far_back, mate_back,
    load_sem, scale_sem, far_send_sem, far_recv_sem, relay_send_sem, relay_recv_sem, mate_send_sem, mate_recv_sem,
    part_send_sem, part_recv_sem, mpart_send_sem, mpart_recv_sem,
):
    chunks = p_ref.shape[0] // CHUNK
    cols = v_ref.shape[0]
    strips, lanes = CHUNK // STRIP, CHUNK // 128
    me = lax.axis_index(AXIS)
    odd = lax.rem(me, 2)
    even = odd == 0
    up, down = lax.rem(me + 2, n), lax.rem(me + n - 2, n)
    mate = me + 1 - 2 * odd
    host = jnp.where(even, down, up)
    guest = jnp.where(even, up, down)

    even_i = 1 - odd
    place_in = lax.rem(me, 8)
    relayed = n % 8 == 0
    source = jnp.logical_and(relayed, jnp.logical_or(place_in == 3, place_in == 4))
    relay = jnp.logical_and(relayed, jnp.logical_or(place_in == 1, place_in == 6))
    target = jnp.logical_and(relayed, jnp.logical_or(place_in == 2, place_in == 5))
    host_two = lax.rem(me + 4 * odd + (n - 4) * even_i, n)
    guest_two = lax.rem(me + 4 * even_i + (n - 4) * odd, n)

    barrier = pltpu.get_barrier_semaphore()

    def load_parts(c):
        pairs = [(p_ref.at[c * CHUNK : (c + 1) * CHUNK], send.at[c, 0:CHUNK])]
        for q in range(lanes):
            first = c * CHUNK + q * 128
            at = CHUNK + q * cols
            pairs.append((v_ref.at[:, first : first + 128], send.at[c, at : at + cols]))
        return [
            pltpu.make_async_copy(src, dst, load_sem.at[c, i])
            for i, (src, dst) in enumerate(pairs)
        ]

    loads = [load_parts(c) for c in range(chunks)]
    scale_load = pltpu.make_async_copy(s_ref, scale_in, scale_sem)
    scale_load.start()
    for group in loads:
        for copy in group:
            copy.start()
    first_sender = jnp.where(target, guest_two, guest)
    for other in (mate, first_sender):
        pl.semaphore_signal(barrier, inc=1, device_id=(other,), device_id_type=MESH)

    @pl.when(relay)
    def _():
        pl.semaphore_signal(barrier, inc=1, device_id=(host,), device_id_type=MESH)

    def place(slot, c, source):
        rows = pl.ds(pl.multiple_of(c * CHUNK, CHUNK), CHUNK)
        pieces = [source[c, CHUNK + q * cols : CHUNK + (q + 1) * cols] for q in range(lanes)]
        high, low = split(source[c, :CHUNK])
        left[slot, c] = jnp.concatenate([high, low, high, low], axis=1)
        right[slot, rows] = jnp.concatenate([high, low, low, high], axis=1)
        held = high.astype(F32) + low.astype(F32)
        squares = held * held
        sq_col[slot, c] = jnp.broadcast_to(
            -0.5 * jnp.sum(squares, axis=1, keepdims=True), (CHUNK, 128)
        )
        row = -0.5 * jnp.sum(squares.T, axis=0, keepdims=True)
        sq_row[slot, :, rows] = jnp.broadcast_to(row, (8, CHUNK))
        vt = jnp.concatenate(pieces, axis=1)
        vec_t[slot, c] = jnp.concatenate(split(vt), axis=0)
        vec[slot, rows] = jnp.concatenate(split(vt.T), axis=1)

    scale_load.wait()
    scale = scale_in[...] * LOG2E_ROOT
    for c in range(chunks):
        for copy in loads[c]:
            copy.wait()
        send[c, :CHUNK] = send[c, :CHUNK] * scale
    pl.semaphore_wait(barrier, 2 + relay.astype(jnp.int32))

    def far_copy(c):
        return pltpu.make_async_remote_copy(
            src_ref=send.at[c], dst_ref=far_in.at[c],
            send_sem=far_send_sem.at[c], recv_sem=far_recv_sem.at[c],
            device_id=(host,), device_id_type=MESH,
        )

    def source_copy(c):
        return pltpu.make_async_remote_copy(
            src_ref=send.at[c], dst_ref=relay_in.at[c],
            send_sem=far_send_sem.at[c], recv_sem=relay_recv_sem.at[c],
            device_id=(guest,), device_id_type=MESH,
        )

    def relay_copy(c):
        return pltpu.make_async_remote_copy(
            src_ref=relay_in.at[c], dst_ref=far_in.at[c],
            send_sem=relay_send_sem.at[c], recv_sem=far_recv_sem.at[c],
            device_id=(host_two,), device_id_type=MESH,
        )

    def send_far(c):
        @pl.when(source)
        def _():
            source_copy(c).start()

        @pl.when(jnp.logical_not(source))
        def _():
            far_copy(c).start()

    def pass_on(c):
        source_copy(c).wait_recv()
        relay_copy(c).start()

    def part_copy(c):
        return pltpu.make_async_remote_copy(
            src_ref=far_part.at[c], dst_ref=far_back.at[c],
            send_sem=part_send_sem.at[c], recv_sem=part_recv_sem.at[c],
            device_id=(guest,), device_id_type=MESH,
        )

    mate_copy = pltpu.make_async_remote_copy(
        src_ref=send, dst_ref=mate_in, send_sem=mate_send_sem, recv_sem=mate_recv_sem,
        device_id=(mate,), device_id_type=MESH,
    )
    mpart_copy = pltpu.make_async_remote_copy(
        src_ref=mate_part, dst_ref=mate_back, send_sem=mpart_send_sem,
        recv_sem=mpart_recv_sem, device_id=(mate,), device_id_type=MESH,
    )
    @pl.when(odd == 1)
    def _():
        for c in range(chunks):
            send_far(c)

    mate_copy.start()

    def place_own(c, carry):
        place(OWN, c, send)
        return carry

    lax.fori_loop(0, chunks, place_own, 0)
    acc_t[...] = jnp.zeros_like(acc_t)

    def fill(a, c, b, first):
        col = jnp.concatenate([sq_col[a, c]] * (STRIP // 128), axis=1)
        cross[:, first:] = dot_nt(left[a, c], right[b, first:])
        for start in range(first, chunks * CHUNK, STRIP):
            at = slice(start, start + STRIP)
            values = jnp.exp2(cross[:, at] + col + sq_row[b, 0:1, at])
            tile_high[:, at], tile_low[:, at] = split(values)
        total = dot(tile_high[:, first:], vec[b, first:]) + dot(tile_low[:, first:], vec[b, first:])
        return fold(total.T)

    def mirror(a, c, b, first):
        acc_t[b, :, first:] += dot(vec_t[a, c], tile_high[:, first:]) + dot(
            vec_t[a, c], tile_low[:, first:]
        )

    def tile(a, c, b):
        part = fill(a, c, b, 0)
        mirror(a, c, b, 0)
        return part

    for c in range(chunks):
        out_t[c] = fill(OWN, c, OWN, c * CHUNK)
        if c + 1 < chunks:
            mirror(OWN, c, OWN, (c + 1) * CHUNK)

        @pl.when(even)
        def _():
            send_far(c)

        @pl.when(jnp.logical_and(relay, odd == 1))
        def _():
            pass_on(c)

    mate_copy.wait_recv()

    def place_mate(c, carry):
        place(MATE, c, mate_in)
        return carry

    lax.fori_loop(0, chunks, place_mate, 0)

    def step(k, carry):
        second = lax.rem(k, 2)
        c = jnp.where(even, lax.rem(k, chunks), lax.div(k, 2))
        uses_far = jnp.logical_or(odd == 1, k >= chunks)
        a = jnp.where(uses_far, FAR, MATE)
        b = jnp.where(even, OWN, jnp.where(second == 0, MATE, OWN))
        arrives = jnp.where(even, k >= chunks, second == 0)

        @pl.when(arrives)
        def _():
            far_copy(c).wait_recv()
            place(FAR, c, far_in)

        part = tile(a, c, b)

        @pl.when(jnp.logical_not(uses_far))
        def _():
            mate_part[c] = part

        @pl.when(jnp.logical_and(uses_far, arrives))
        def _():
            far_part[c] = part

        @pl.when(jnp.logical_and(uses_far, jnp.logical_not(arrives)))
        def _():
            far_part[c] += part

        @pl.when(jnp.where(even, k >= chunks, second == 1))
        def _():
            part_copy(c).start()

        @pl.when(jnp.logical_and(jnp.logical_and(relay, even), k < chunks))
        def _():
            pass_on(c)

        @pl.when(jnp.logical_and(even, k == chunks - 1))
        def _():
            mpart_copy.start()

        return carry

    lax.fori_loop(0, 2 * chunks, step, 0)

    def mirror_of(b, c):
        return fold(acc_t[b, :, c * CHUNK : (c + 1) * CHUNK])

    @pl.when(odd == 1)
    def _():
        for c in range(chunks):
            mate_part[c] = mirror_of(MATE, c)
        mpart_copy.start()

    for c in range(chunks):
        out_t[c] += mirror_of(OWN, c)
    mpart_copy.wait_recv()
    for c in range(chunks):
        part_copy(c).wait_recv()
        o_ref[:, c * CHUNK : (c + 1) * CHUNK] = out_t[c] + mate_back[c] + far_back[c]
    for c in range(chunks):
        far_copy(c).wait_send()
        part_copy(c).wait_send()

    @pl.when(relay)
    def _():
        for c in range(chunks):
            relay_copy(c).wait_send()

    mate_copy.wait_send()
    mpart_copy.wait_send()


def per_device(points, inv_scale, vectors):
    n = lax.axis_size(AXIS)
    rows, feat = points.shape
    cols = vectors.shape[1]
    chunks = rows // CHUNK
    packed = (chunks, CHUNK + CHUNK // 128 * cols, 128)
    turned = (chunks, cols, CHUNK)
    vmem = pl.BlockSpec(memory_space=pltpu.VMEM)
    sem = pltpu.SemaphoreType.DMA
    return pl.pallas_call(
        functools.partial(kernel, n),
        out_shape=jax.ShapeDtypeStruct((cols, rows), F32),
        in_specs=[pl.BlockSpec(memory_space=pltpu.HBM)] * 3,
        out_specs=vmem,
        scratch_shapes=[
            pltpu.VMEM(packed, F32),
            pltpu.VMEM(packed, F32),
            pltpu.VMEM(packed, F32),
            pltpu.VMEM(packed, F32),
            pltpu.VMEM((3, chunks, CHUNK, 4 * feat), BF16),
            pltpu.VMEM((3, rows, 4 * feat), BF16),
            pltpu.VMEM((3, rows, 2 * cols), BF16),
            pltpu.VMEM((3, chunks, 2 * cols, CHUNK), BF16),
            pltpu.VMEM((3, chunks, CHUNK, 128), F32),
            pltpu.VMEM((3, 8, rows), F32),
            pltpu.VMEM((2, 2 * cols, rows), F32),
            pltpu.VMEM(turned, F32),
            pltpu.VMEM((CHUNK, rows), F32),
            pltpu.VMEM((CHUNK, rows), BF16),
            pltpu.VMEM((CHUNK, rows), BF16),
            pltpu.VMEM((1, feat), F32),
            pltpu.VMEM(turned, F32),
            pltpu.VMEM(turned, F32),
            pltpu.VMEM(turned, F32),
            pltpu.VMEM(turned, F32),
            sem((chunks, 1 + CHUNK // 128)), sem,
            sem((chunks,)), sem((chunks,)), sem((chunks,)), sem((chunks,)), sem, sem,
            sem((chunks,)), sem((chunks,)), sem, sem,
        ],
        compiler_params=pltpu.CompilerParams(
            collective_id=0, has_side_effects=True, vmem_limit_bytes=64 * 1024 * 1024 - 512 * 1024
        ),
    )(points, inv_scale[None, :], vectors.T).T


def solution(mesh):
    return jax.shard_map(
        per_device, mesh=mesh,
        in_specs=(P(AXIS, None), P(), P(AXIS, None)), out_specs=P(AXIS, None),
        check_vma=False,
    )
```

```python
import functools

import jax
import jax.numpy as jnp
from jax import lax
from jax.experimental import pallas as pl
from jax.experimental.pallas import tpu as pltpu
from jax.sharding import PartitionSpec as P

AXIS = "blk"
CHUNK = 512
STRIP = 256
LOG2E_ROOT = 1.2011224087864498
OWN, MATE, FAR = 0, 1, 2
MESH = pl.DeviceIdType.MESH
F32, BF16 = jnp.float32, jnp.bfloat16


def split(x):
    high = x.astype(BF16)
    return high, (x - high.astype(F32)).astype(BF16)


def dot(a, b):
    return lax.dot_general(a, b, (((1,), (0,)), ((), ())), preferred_element_type=F32)


def dot_nt(a, b):
    return lax.dot_general(a, b, (((1,), (1,)), ((), ())), preferred_element_type=F32)


def fold(wide):
    half = wide.shape[0] // 2
    return wide[:half] + wide[half:]


def kernel(
    n, p_ref, s_ref, v_ref, o_ref,
    send, far_in, mate_in, left, right, vec, vec_t, sq_col, sq_row, acc_t, out_t,
    cross, tile_high, tile_low, scale_in,
    far_part, mate_part, far_back, mate_back,
    load_sem, scale_sem, far_send_sem, far_recv_sem, mate_send_sem, mate_recv_sem,
    part_send_sem, part_recv_sem, mpart_send_sem, mpart_recv_sem,
):
    chunks = p_ref.shape[0] // CHUNK
    cols = v_ref.shape[0]
    strips, lanes = CHUNK // STRIP, CHUNK // 128
    me = lax.axis_index(AXIS)
    odd = lax.rem(me, 2)
    even = odd == 0
    up, down = lax.rem(me + 2, n), lax.rem(me + n - 2, n)
    mate = me + 1 - 2 * odd
    host = jnp.where(even, down, up)
    guest = jnp.where(even, up, down)

    barrier = pltpu.get_barrier_semaphore()

    def load_parts(c):
        pairs = [(p_ref.at[c * CHUNK : (c + 1) * CHUNK], send.at[c, 0:CHUNK])]
        for q in range(lanes):
            first = c * CHUNK + q * 128
            at = CHUNK + q * cols
            pairs.append((v_ref.at[:, first : first + 128], send.at[c, at : at + cols]))
        return [
            pltpu.make_async_copy(src, dst, load_sem.at[c, i])
            for i, (src, dst) in enumerate(pairs)
        ]

    loads = [load_parts(c) for c in range(chunks)]
    scale_load = pltpu.make_async_copy(s_ref, scale_in, scale_sem)
    scale_load.start()
    for group in loads:
        for copy in group:
            copy.start()
    for other in (mate, guest):
        pl.semaphore_signal(barrier, inc=1, device_id=(other,), device_id_type=MESH)

    def place(slot, c, source):
        rows = pl.ds(pl.multiple_of(c * CHUNK, CHUNK), CHUNK)
        pieces = [source[c, CHUNK + q * cols : CHUNK + (q + 1) * cols] for q in range(lanes)]
        high, low = split(source[c, :CHUNK])
        left[slot, c] = jnp.concatenate([high, low, high, low], axis=1)
        right[slot, rows] = jnp.concatenate([high, low, low, high], axis=1)
        held = high.astype(F32) + low.astype(F32)
        squares = held * held
        sq_col[slot, c] = jnp.broadcast_to(
            -0.5 * jnp.sum(squares, axis=1, keepdims=True), (CHUNK, 128)
        )
        row = -0.5 * jnp.sum(squares.T, axis=0, keepdims=True)
        sq_row[slot, :, rows] = jnp.broadcast_to(row, (8, CHUNK))
        vt = jnp.concatenate(pieces, axis=1)
        vec_t[slot, c] = jnp.concatenate(split(vt), axis=0)
        vec[slot, rows] = jnp.concatenate(split(vt.T), axis=1)

    scale_load.wait()
    scale = scale_in[...] * LOG2E_ROOT
    for c in range(chunks):
        for copy in loads[c]:
            copy.wait()
        send[c, :CHUNK] = send[c, :CHUNK] * scale
    pl.semaphore_wait(barrier, 2)

    def far_copy(c):
        return pltpu.make_async_remote_copy(
            src_ref=send.at[c], dst_ref=far_in.at[c],
            send_sem=far_send_sem.at[c], recv_sem=far_recv_sem.at[c],
            device_id=(host,), device_id_type=MESH,
        )

    def part_copy(c):
        return pltpu.make_async_remote_copy(
            src_ref=far_part.at[c], dst_ref=far_back.at[c],
            send_sem=part_send_sem.at[c], recv_sem=part_recv_sem.at[c],
            device_id=(guest,), device_id_type=MESH,
        )

    mate_copy = pltpu.make_async_remote_copy(
        src_ref=send, dst_ref=mate_in, send_sem=mate_send_sem, recv_sem=mate_recv_sem,
        device_id=(mate,), device_id_type=MESH,
    )
    mpart_copy = pltpu.make_async_remote_copy(
        src_ref=mate_part, dst_ref=mate_back, send_sem=mpart_send_sem,
        recv_sem=mpart_recv_sem, device_id=(mate,), device_id_type=MESH,
    )
    @pl.when(odd == 1)
    def _():
        far_copy(0).start()

    mate_copy.start()

    def place_own(c, carry):
        place(OWN, c, send)
        return carry

    lax.fori_loop(0, chunks, place_own, 0)
    acc_t[...] = jnp.zeros_like(acc_t)

    def fill(a, c, b, first):
        col = jnp.concatenate([sq_col[a, c]] * (STRIP // 128), axis=1)
        cross[:, first:] = dot_nt(left[a, c], right[b, first:])
        for start in range(first, chunks * CHUNK, STRIP):
            at = slice(start, start + STRIP)
            values = jnp.exp2(cross[:, at] + col + sq_row[b, 0:1, at])
            tile_high[:, at], tile_low[:, at] = split(values)
        total = dot(tile_high[:, first:], vec[b, first:]) + dot(tile_low[:, first:], vec[b, first:])
        return fold(total.T)

    def mirror(a, c, b, first):
        acc_t[b, :, first:] += dot(vec_t[a, c], tile_high[:, first:]) + dot(
            vec_t[a, c], tile_low[:, first:]
        )

    def tile(a, c, b):
        part = fill(a, c, b, 0)
        mirror(a, c, b, 0)
        return part

    for c in range(chunks):
        out_t[c] = fill(OWN, c, OWN, c * CHUNK)
        if c + 1 < chunks:
            mirror(OWN, c, OWN, (c + 1) * CHUNK)

        @pl.when(jnp.logical_and(odd == 1, c + 1 < chunks))
        def _():
            far_copy(min(c + 1, chunks - 1)).start()

        @pl.when(jnp.logical_and(even, c >= 1))
        def _():
            far_copy(max(c - 1, 0)).start()

    mate_copy.wait_recv()

    def place_mate(c, carry):
        place(MATE, c, mate_in)
        return carry

    lax.fori_loop(0, chunks, place_mate, 0)

    def step(k, carry):
        second = lax.rem(k, 2)
        c = jnp.where(even, lax.rem(k, chunks), lax.div(k, 2))
        uses_far = jnp.logical_or(odd == 1, k >= chunks)
        a = jnp.where(uses_far, FAR, MATE)
        b = jnp.where(even, OWN, jnp.where(second == 0, MATE, OWN))
        arrives = jnp.where(even, k >= chunks, second == 0)

        @pl.when(arrives)
        def _():
            far_copy(c).wait_recv()
            place(FAR, c, far_in)

        part = tile(a, c, b)

        @pl.when(jnp.logical_not(uses_far))
        def _():
            mate_part[c] = part

        @pl.when(jnp.logical_and(uses_far, arrives))
        def _():
            far_part[c] = part

        @pl.when(jnp.logical_and(uses_far, jnp.logical_not(arrives)))
        def _():
            far_part[c] += part

        @pl.when(jnp.where(even, k >= chunks, second == 1))
        def _():
            part_copy(c).start()

        @pl.when(jnp.logical_and(even, k == 0))
        def _():
            far_copy(chunks - 1).start()

        @pl.when(jnp.logical_and(even, k == chunks - 1))
        def _():
            mpart_copy.start()

        return carry

    lax.fori_loop(0, 2 * chunks, step, 0)

    def mirror_of(b, c):
        return fold(acc_t[b, :, c * CHUNK : (c + 1) * CHUNK])

    @pl.when(odd == 1)
    def _():
        for c in range(chunks):
            mate_part[c] = mirror_of(MATE, c)
        mpart_copy.start()

    for c in range(chunks):
        out_t[c] += mirror_of(OWN, c)
    mpart_copy.wait_recv()
    for c in range(chunks):
        part_copy(c).wait_recv()
        o_ref[:, c * CHUNK : (c + 1) * CHUNK] = out_t[c] + mate_back[c] + far_back[c]
    for c in range(chunks):
        far_copy(c).wait_send()
        part_copy(c).wait_send()
    mate_copy.wait_send()
    mpart_copy.wait_send()


def per_device(points, inv_scale, vectors):
    n = lax.axis_size(AXIS)
    rows, feat = points.shape
    cols = vectors.shape[1]
    chunks = rows // CHUNK
    packed = (chunks, CHUNK + CHUNK // 128 * cols, 128)
    turned = (chunks, cols, CHUNK)
    vmem = pl.BlockSpec(memory_space=pltpu.VMEM)
    sem = pltpu.SemaphoreType.DMA
    return pl.pallas_call(
        functools.partial(kernel, n),
        out_shape=jax.ShapeDtypeStruct((cols, rows), F32),
        in_specs=[pl.BlockSpec(memory_space=pltpu.HBM)] * 3,
        out_specs=vmem,
        scratch_shapes=[
            pltpu.VMEM(packed, F32),
            pltpu.VMEM(packed, F32),
            pltpu.VMEM(packed, F32),
            pltpu.VMEM((3, chunks, CHUNK, 4 * feat), BF16),
            pltpu.VMEM((3, rows, 4 * feat), BF16),
            pltpu.VMEM((3, rows, 2 * cols), BF16),
            pltpu.VMEM((3, chunks, 2 * cols, CHUNK), BF16),
            pltpu.VMEM((3, chunks, CHUNK, 128), F32),
            pltpu.VMEM((3, 8, rows), F32),
            pltpu.VMEM((2, 2 * cols, rows), F32),
            pltpu.VMEM(turned, F32),
            pltpu.VMEM((CHUNK, rows), F32),
            pltpu.VMEM((CHUNK, rows), BF16),
            pltpu.VMEM((CHUNK, rows), BF16),
            pltpu.VMEM((1, feat), F32),
            pltpu.VMEM(turned, F32),
            pltpu.VMEM(turned, F32),
            pltpu.VMEM(turned, F32),
            pltpu.VMEM(turned, F32),
            sem((chunks, 1 + CHUNK // 128)), sem,
            sem((chunks,)), sem((chunks,)), sem, sem,
            sem((chunks,)), sem((chunks,)), sem, sem,
        ],
        compiler_params=pltpu.CompilerParams(
            collective_id=0, has_side_effects=True, vmem_limit_bytes=64 * 1024 * 1024 - 8192 * 1024
        ),
    )(points, inv_scale[None, :], vectors.T).T


def solution(mesh):
    return jax.shard_map(
        per_device, mesh=mesh,
        in_specs=(P(AXIS, None), P(), P(AXIS, None)), out_specs=P(AXIS, None),
        check_vma=False,
    )
```

```python
import functools

import jax
import jax.numpy as jnp
from jax import lax
from jax.experimental import pallas as pl
from jax.experimental.pallas import tpu as pltpu
from jax.sharding import PartitionSpec as P

AXIS = "blk"
CHUNK = 512
STRIP = 256
LOG2E_ROOT = 1.2011224087864498
OWN, MATE, FAR = 0, 1, 2
MESH = pl.DeviceIdType.MESH
F32, BF16 = jnp.float32, jnp.bfloat16


def split(x):
    high = x.astype(BF16)
    return high, (x - high.astype(F32)).astype(BF16)


def dot(a, b):
    return lax.dot_general(a, b, (((1,), (0,)), ((), ())), preferred_element_type=F32)


def dot_nt(a, b):
    return lax.dot_general(a, b, (((1,), (1,)), ((), ())), preferred_element_type=F32)


def fold(wide):
    half = wide.shape[0] // 2
    return wide[:half] + wide[half:]


def kernel(
    n, p_ref, s_ref, v_ref, o_ref,
    send, far_in, mate_in, left, right, vec, vec_t, sq_col, sq_row, acc_t, out_t,
    cross, tile_high, tile_low, scale_in,
    far_part, mate_part, far_back, mate_back,
    load_sem, scale_sem, far_send_sem, far_recv_sem, mate_send_sem, mate_recv_sem,
    part_send_sem, part_recv_sem, mpart_send_sem, mpart_recv_sem,
):
    chunks = p_ref.shape[0] // CHUNK
    cols = v_ref.shape[0]
    strips, lanes = CHUNK // STRIP, CHUNK // 128
    me = lax.axis_index(AXIS)
    odd = lax.rem(me, 2)
    even = odd == 0
    up, down = lax.rem(me + 2, n), lax.rem(me + n - 2, n)
    mate = me + 1 - 2 * odd
    host = jnp.where(even, down, up)
    guest = jnp.where(even, up, down)

    barrier = pltpu.get_barrier_semaphore()

    def load_parts(c):
        pairs = [(p_ref.at[c * CHUNK : (c + 1) * CHUNK], send.at[c, 0:CHUNK])]
        for q in range(lanes):
            first = c * CHUNK + q * 128
            at = CHUNK + q * cols
            pairs.append((v_ref.at[:, first : first + 128], send.at[c, at : at + cols]))
        return [
            pltpu.make_async_copy(src, dst, load_sem.at[c, i])
            for i, (src, dst) in enumerate(pairs)
        ]

    loads = [load_parts(c) for c in range(chunks)]
    scale_load = pltpu.make_async_copy(s_ref, scale_in, scale_sem)
    scale_load.start()
    for group in loads:
        for copy in group:
            copy.start()
    for other in (mate, guest):
        pl.semaphore_signal(barrier, inc=1, device_id=(other,), device_id_type=MESH)

    def place(slot, c, source):
        rows = pl.ds(pl.multiple_of(c * CHUNK, CHUNK), CHUNK)
        pieces = [source[c, CHUNK + q * cols : CHUNK + (q + 1) * cols] for q in range(lanes)]
        high, low = split(source[c, :CHUNK])
        left[slot, c] = jnp.concatenate([high, low, high, low], axis=1)
        right[slot, rows] = jnp.concatenate([high, low, low, high], axis=1)
        held = high.astype(F32) + low.astype(F32)
        squares = held * held
        sq_col[slot, c] = jnp.broadcast_to(
            -0.5 * jnp.sum(squares, axis=1, keepdims=True), (CHUNK, 128)
        )
        row = -0.5 * jnp.sum(squares.T, axis=0, keepdims=True)
        sq_row[slot, :, rows] = jnp.broadcast_to(row, (8, CHUNK))
        vt = jnp.concatenate(pieces, axis=1)
        vec_t[slot, c] = jnp.concatenate(split(vt), axis=0)
        vec[slot, rows] = jnp.concatenate(split(vt.T), axis=1)

    scale_load.wait()
    scale = scale_in[...] * LOG2E_ROOT
    for c in range(chunks):
        for copy in loads[c]:
            copy.wait()
        send[c, :CHUNK] = send[c, :CHUNK] * scale
    pl.semaphore_wait(barrier, 2)

    def far_copy(c):
        return pltpu.make_async_remote_copy(
            src_ref=send.at[c], dst_ref=far_in.at[c],
            send_sem=far_send_sem.at[c], recv_sem=far_recv_sem.at[c],
            device_id=(host,), device_id_type=MESH,
        )

    def part_copy(c):
        return pltpu.make_async_remote_copy(
            src_ref=far_part.at[c], dst_ref=far_back.at[c],
            send_sem=part_send_sem.at[c], recv_sem=part_recv_sem.at[c],
            device_id=(guest,), device_id_type=MESH,
        )

    mate_copy = pltpu.make_async_remote_copy(
        src_ref=send, dst_ref=mate_in, send_sem=mate_send_sem, recv_sem=mate_recv_sem,
        device_id=(mate,), device_id_type=MESH,
    )
    mpart_copy = pltpu.make_async_remote_copy(
        src_ref=mate_part, dst_ref=mate_back, send_sem=mpart_send_sem,
        recv_sem=mpart_recv_sem, device_id=(mate,), device_id_type=MESH,
    )
    @pl.when(odd == 1)
    def _():
        far_copy(0).start()

    mate_copy.start()

    def place_own(c, carry):
        place(OWN, c, send)
        return carry

    lax.fori_loop(0, chunks, place_own, 0)
    acc_t[...] = jnp.zeros_like(acc_t)

    def fill(a, c, b, first):
        col = jnp.concatenate([sq_col[a, c]] * (STRIP // 128), axis=1)
        cross[:, first:] = dot_nt(left[a, c], right[b, first:])
        for start in range(first, chunks * CHUNK, STRIP):
            at = slice(start, start + STRIP)
            values = jnp.exp2(cross[:, at] + col + sq_row[b, 0:1, at])
            tile_high[:, at], tile_low[:, at] = split(values)
        total = dot(tile_high[:, first:], vec[b, first:]) + dot(tile_low[:, first:], vec[b, first:])
        return fold(total.T)

    def mirror(a, c, b, first):
        acc_t[b, :, first:] += dot(vec_t[a, c], tile_high[:, first:]) + dot(
            vec_t[a, c], tile_low[:, first:]
        )

    def tile(a, c, b):
        part = fill(a, c, b, 0)
        mirror(a, c, b, 0)
        return part

    for c in range(chunks):
        out_t[c] = fill(OWN, c, OWN, c * CHUNK)
        if c + 1 < chunks:
            mirror(OWN, c, OWN, (c + 1) * CHUNK)

        @pl.when(jnp.logical_and(odd == 1, c + 1 < chunks))
        def _():
            far_copy(min(c + 1, chunks - 1)).start()

        @pl.when(even)
        def _():
            far_copy(c).start()

    mate_copy.wait_recv()

    def place_mate(c, carry):
        place(MATE, c, mate_in)
        return carry

    lax.fori_loop(0, chunks, place_mate, 0)

    def step(k, carry):
        second = lax.rem(k, 2)
        c = jnp.where(even, lax.rem(k, chunks), lax.div(k, 2))
        uses_far = jnp.logical_or(odd == 1, k >= chunks)
        a = jnp.where(uses_far, FAR, MATE)
        b = jnp.where(even, OWN, jnp.where(second == 0, MATE, OWN))
        arrives = jnp.where(even, k >= chunks, second == 0)

        @pl.when(arrives)
        def _():
            far_copy(c).wait_recv()
            place(FAR, c, far_in)

        part = tile(a, c, b)

        @pl.when(jnp.logical_not(uses_far))
        def _():
            mate_part[c] = part

        @pl.when(jnp.logical_and(uses_far, arrives))
        def _():
            far_part[c] = part

        @pl.when(jnp.logical_and(uses_far, jnp.logical_not(arrives)))
        def _():
            far_part[c] += part

        @pl.when(jnp.where(even, k >= chunks, second == 1))
        def _():
            part_copy(c).start()

        @pl.when(jnp.logical_and(even, k == chunks - 1))
        def _():
            mpart_copy.start()

        return carry

    lax.fori_loop(0, 2 * chunks, step, 0)

    def mirror_of(b, c):
        return fold(acc_t[b, :, c * CHUNK : (c + 1) * CHUNK])

    @pl.when(odd == 1)
    def _():
        for c in range(chunks):
            mate_part[c] = mirror_of(MATE, c)
        mpart_copy.start()

    for c in range(chunks):
        out_t[c] += mirror_of(OWN, c)
    mpart_copy.wait_recv()
    for c in range(chunks):
        part_copy(c).wait_recv()
        o_ref[:, c * CHUNK : (c + 1) * CHUNK] = out_t[c] + mate_back[c] + far_back[c]
    for c in range(chunks):
        far_copy(c).wait_send()
        part_copy(c).wait_send()
    mate_copy.wait_send()
    mpart_copy.wait_send()


def per_device(points, inv_scale, vectors):
    n = lax.axis_size(AXIS)
    rows, feat = points.shape
    cols = vectors.shape[1]
    chunks = rows // CHUNK
    packed = (chunks, CHUNK + CHUNK // 128 * cols, 128)
    turned = (chunks, cols, CHUNK)
    vmem = pl.BlockSpec(memory_space=pltpu.VMEM)
    sem = pltpu.SemaphoreType.DMA
    return pl.pallas_call(
        functools.partial(kernel, n),
        out_shape=jax.ShapeDtypeStruct((cols, rows), F32),
        in_specs=[pl.BlockSpec(memory_space=pltpu.HBM)] * 3,
        out_specs=vmem,
        scratch_shapes=[
            pltpu.VMEM(packed, F32),
            pltpu.VMEM(packed, F32),
            pltpu.VMEM(packed, F32),
            pltpu.VMEM((3, chunks, CHUNK, 4 * feat), BF16),
            pltpu.VMEM((3, rows, 4 * feat), BF16),
            pltpu.VMEM((3, rows, 2 * cols), BF16),
            pltpu.VMEM((3, chunks, 2 * cols, CHUNK), BF16),
            pltpu.VMEM((3, chunks, CHUNK, 128), F32),
            pltpu.VMEM((3, 8, rows), F32),
            pltpu.VMEM((2, 2 * cols, rows), F32),
            pltpu.VMEM(turned, F32),
            pltpu.VMEM((CHUNK, rows), F32),
            pltpu.VMEM((CHUNK, rows), BF16),
            pltpu.VMEM((CHUNK, rows), BF16),
            pltpu.VMEM((1, feat), F32),
            pltpu.VMEM(turned, F32),
            pltpu.VMEM(turned, F32),
            pltpu.VMEM(turned, F32),
            pltpu.VMEM(turned, F32),
            sem((chunks, 1 + CHUNK // 128)), sem,
            sem((chunks,)), sem((chunks,)), sem, sem,
            sem((chunks,)), sem((chunks,)), sem, sem,
        ],
        compiler_params=pltpu.CompilerParams(
            collective_id=0, has_side_effects=True, vmem_limit_bytes=64 * 1024 * 1024 - 8192 * 1024
        ),
    )(points, inv_scale[None, :], vectors.T).T


def solution(mesh):
    return jax.shard_map(
        per_device, mesh=mesh,
        in_specs=(P(AXIS, None), P(), P(AXIS, None)), out_specs=P(AXIS, None),
        check_vma=False,
    )
```

```python
import functools

import jax
import jax.numpy as jnp
from jax import lax
from jax.experimental import pallas as pl
from jax.experimental.pallas import tpu as pltpu
from jax.sharding import PartitionSpec as P

AXIS = "blk"
CHUNK = 512
STRIP = 256
LOG2E_ROOT = 1.2011224087864498
OWN, MATE, FAR = 0, 1, 2
MESH = pl.DeviceIdType.MESH
F32, BF16 = jnp.float32, jnp.bfloat16


def split(x):
    high = x.astype(BF16)
    return high, (x - high.astype(F32)).astype(BF16)


def dot(a, b):
    return lax.dot_general(a, b, (((1,), (0,)), ((), ())), preferred_element_type=F32)


def dot_nt(a, b):
    return lax.dot_general(a, b, (((1,), (1,)), ((), ())), preferred_element_type=F32)


def fold(wide):
    half = wide.shape[0] // 2
    return wide[:half] + wide[half:]


def kernel(
    n, p_ref, s_ref, v_ref, o_ref,
    send, far_in, mate_in, left, right, vec, vec_t, sq_col, sq_row, acc_t, out_t,
    cross, tile_high, tile_low, scale_in,
    far_part, mate_part, far_back, mate_back,
    load_sem, scale_sem, far_send_sem, far_recv_sem, mate_send_sem, mate_recv_sem,
    part_send_sem, part_recv_sem, mpart_send_sem, mpart_recv_sem,
):
    chunks = p_ref.shape[0] // CHUNK
    cols = v_ref.shape[0]
    strips, lanes = CHUNK // STRIP, CHUNK // 128
    me = lax.axis_index(AXIS)
    odd = lax.rem(me, 2)
    even = odd == 0
    up, down = lax.rem(me + 2, n), lax.rem(me + n - 2, n)
    mate = me + 1 - 2 * odd
    host = jnp.where(even, down, up)
    guest = jnp.where(even, up, down)

    barrier = pltpu.get_barrier_semaphore()

    def load_parts(c):
        pairs = [(p_ref.at[c * CHUNK : (c + 1) * CHUNK], send.at[c, 0:CHUNK])]
        for q in range(lanes):
            first = c * CHUNK + q * 128
            at = CHUNK + q * cols
            pairs.append((v_ref.at[:, first : first + 128], send.at[c, at : at + cols]))
        return [
            pltpu.make_async_copy(src, dst, load_sem.at[c, i])
            for i, (src, dst) in enumerate(pairs)
        ]

    loads = [load_parts(c) for c in range(chunks)]
    scale_load = pltpu.make_async_copy(s_ref, scale_in, scale_sem)
    scale_load.start()
    for group in loads:
        for copy in group:
            copy.start()
    for other in (mate, guest):
        pl.semaphore_signal(barrier, inc=1, device_id=(other,), device_id_type=MESH)

    def place(slot, c, source):
        rows = pl.ds(pl.multiple_of(c * CHUNK, CHUNK), CHUNK)
        pieces = [source[c, CHUNK + q * cols : CHUNK + (q + 1) * cols] for q in range(lanes)]
        high, low = split(source[c, :CHUNK])
        left[slot, c] = jnp.concatenate([high, low, high, low], axis=1)
        right[slot, rows] = jnp.concatenate([high, low, low, high], axis=1)
        held = high.astype(F32) + low.astype(F32)
        squares = held * held
        sq_col[slot, c] = jnp.broadcast_to(
            -0.5 * jnp.sum(squares, axis=1, keepdims=True), (CHUNK, 128)
        )
        row = -0.5 * jnp.sum(squares.T, axis=0, keepdims=True)
        sq_row[slot, :, rows] = jnp.broadcast_to(row, (8, CHUNK))
        vt = jnp.concatenate(pieces, axis=1)
        vec_t[slot, c] = jnp.concatenate(split(vt), axis=0)
        vec[slot, rows] = jnp.concatenate(split(vt.T), axis=1)

    scale_load.wait()
    scale = scale_in[...] * LOG2E_ROOT
    for c in range(chunks):
        for copy in loads[c]:
            copy.wait()
        send[c, :CHUNK] = send[c, :CHUNK] * scale
    pl.semaphore_wait(barrier, 2)

    def far_copy(c):
        return pltpu.make_async_remote_copy(
            src_ref=send.at[c], dst_ref=far_in.at[c],
            send_sem=far_send_sem.at[c], recv_sem=far_recv_sem.at[c],
            device_id=(host,), device_id_type=MESH,
        )

    def part_copy(c):
        return pltpu.make_async_remote_copy(
            src_ref=far_part.at[c], dst_ref=far_back.at[c],
            send_sem=part_send_sem.at[c], recv_sem=part_recv_sem.at[c],
            device_id=(guest,), device_id_type=MESH,
        )

    mate_copy = pltpu.make_async_remote_copy(
        src_ref=send, dst_ref=mate_in, send_sem=mate_send_sem, recv_sem=mate_recv_sem,
        device_id=(mate,), device_id_type=MESH,
    )
    mpart_copy = pltpu.make_async_remote_copy(
        src_ref=mate_part, dst_ref=mate_back, send_sem=mpart_send_sem,
        recv_sem=mpart_recv_sem, device_id=(mate,), device_id_type=MESH,
    )
    @pl.when(odd == 1)
    def _():
        for c in range(chunks):
            far_copy(c).start()

    mate_copy.start()

    def place_own(c, carry):
        place(OWN, c, send)
        return carry

    lax.fori_loop(0, chunks, place_own, 0)
    acc_t[...] = jnp.zeros_like(acc_t)

    def fill(a, c, b, first):
        col = jnp.concatenate([sq_col[a, c]] * (STRIP // 128), axis=1)
        cross[:, first:] = dot_nt(left[a, c], right[b, first:])
        for start in range(first, chunks * CHUNK, STRIP):
            at = slice(start, start + STRIP)
            values = jnp.exp2(cross[:, at] + col + sq_row[b, 0:1, at])
            tile_high[:, at], tile_low[:, at] = split(values)
        total = dot(tile_high[:, first:], vec[b, first:]) + dot(tile_low[:, first:], vec[b, first:])
        return fold(total.T)

    def mirror(a, c, b, first):
        acc_t[b, :, first:] += dot(vec_t[a, c], tile_high[:, first:]) + dot(
            vec_t[a, c], tile_low[:, first:]
        )

    def tile(a, c, b):
        part = fill(a, c, b, 0)
        mirror(a, c, b, 0)
        return part

    for c in range(chunks):
        out_t[c] = fill(OWN, c, OWN, c * CHUNK)
        if c + 1 < chunks:
            mirror(OWN, c, OWN, (c + 1) * CHUNK)

        @pl.when(jnp.logical_and(even, c >= 1))
        def _():
            far_copy(max(c - 1, 0)).start()

    mate_copy.wait_recv()

    def place_mate(c, carry):
        place(MATE, c, mate_in)
        return carry

    lax.fori_loop(0, chunks, place_mate, 0)

    def step(k, carry):
        second = lax.rem(k, 2)
        c = jnp.where(even, lax.rem(k, chunks), lax.div(k, 2))
        uses_far = jnp.logical_or(odd == 1, k >= chunks)
        a = jnp.where(uses_far, FAR, MATE)
        b = jnp.where(even, OWN, jnp.where(second == 0, MATE, OWN))
        arrives = jnp.where(even, k >= chunks, second == 0)

        @pl.when(arrives)
        def _():
            far_copy(c).wait_recv()
            place(FAR, c, far_in)

        part = tile(a, c, b)

        @pl.when(jnp.logical_not(uses_far))
        def _():
            mate_part[c] = part

        @pl.when(jnp.logical_and(uses_far, arrives))
        def _():
            far_part[c] = part

        @pl.when(jnp.logical_and(uses_far, jnp.logical_not(arrives)))
        def _():
            far_part[c] += part

        @pl.when(jnp.where(even, k >= chunks, second == 1))
        def _():
            part_copy(c).start()

        @pl.when(jnp.logical_and(even, k == 0))
        def _():
            far_copy(chunks - 1).start()

        @pl.when(jnp.logical_and(even, k == chunks - 1))
        def _():
            mpart_copy.start()

        return carry

    lax.fori_loop(0, 2 * chunks, step, 0)

    def mirror_of(b, c):
        return fold(acc_t[b, :, c * CHUNK : (c + 1) * CHUNK])

    @pl.when(odd == 1)
    def _():
        for c in range(chunks):
            mate_part[c] = mirror_of(MATE, c)
        mpart_copy.start()

    for c in range(chunks):
        out_t[c] += mirror_of(OWN, c)
    mpart_copy.wait_recv()
    for c in range(chunks):
        part_copy(c).wait_recv()
        o_ref[:, c * CHUNK : (c + 1) * CHUNK] = out_t[c] + mate_back[c] + far_back[c]
    for c in range(chunks):
        far_copy(c).wait_send()
        part_copy(c).wait_send()
    mate_copy.wait_send()
    mpart_copy.wait_send()


def per_device(points, inv_scale, vectors):
    n = lax.axis_size(AXIS)
    rows, feat = points.shape
    cols = vectors.shape[1]
    chunks = rows // CHUNK
    packed = (chunks, CHUNK + CHUNK // 128 * cols, 128)
    turned = (chunks, cols, CHUNK)
    vmem = pl.BlockSpec(memory_space=pltpu.VMEM)
    sem = pltpu.SemaphoreType.DMA
    return pl.pallas_call(
        functools.partial(kernel, n),
        out_shape=jax.ShapeDtypeStruct((cols, rows), F32),
        in_specs=[pl.BlockSpec(memory_space=pltpu.HBM)] * 3,
        out_specs=vmem,
        scratch_shapes=[
            pltpu.VMEM(packed, F32),
            pltpu.VMEM(packed, F32),
            pltpu.VMEM(packed, F32),
            pltpu.VMEM((3, chunks, CHUNK, 4 * feat), BF16),
            pltpu.VMEM((3, rows, 4 * feat), BF16),
            pltpu.VMEM((3, rows, 2 * cols), BF16),
            pltpu.VMEM((3, chunks, 2 * cols, CHUNK), BF16),
            pltpu.VMEM((3, chunks, CHUNK, 128), F32),
            pltpu.VMEM((3, 8, rows), F32),
            pltpu.VMEM((2, 2 * cols, rows), F32),
            pltpu.VMEM(turned, F32),
            pltpu.VMEM((CHUNK, rows), F32),
            pltpu.VMEM((CHUNK, rows), BF16),
            pltpu.VMEM((CHUNK, rows), BF16),
            pltpu.VMEM((1, feat), F32),
            pltpu.VMEM(turned, F32),
            pltpu.VMEM(turned, F32),
            pltpu.VMEM(turned, F32),
            pltpu.VMEM(turned, F32),
            sem((chunks, 1 + CHUNK // 128)), sem,
            sem((chunks,)), sem((chunks,)), sem, sem,
            sem((chunks,)), sem((chunks,)), sem, sem,
        ],
        compiler_params=pltpu.CompilerParams(
            collective_id=0, has_side_effects=True, vmem_limit_bytes=64 * 1024 * 1024 - 8192 * 1024
        ),
    )(points, inv_scale[None, :], vectors.T).T


def solution(mesh):
    return jax.shard_map(
        per_device, mesh=mesh,
        in_specs=(P(AXIS, None), P(), P(AXIS, None)), out_specs=P(AXIS, None),
        check_vma=False,
    )
```
